256 devices in a mesh: shot: 16 (over z_hi, x), rcv: 16 (over z_lo, y, core).
Axes of the slice: x: 4, y: 4, z: 8 (z_hi: 4, z_lo: 2; z = z_hi * 2 + z_lo), core: 2. Of those that a mesh axis runs over, the one named last changes fastest.
Arguments:
- spectra: bfloat16 [16, 16384, 2, 1024], P('rcv', 'shot'), may hold values from -6 to 6
- shot_grid: int32 [2, 16384], P(None, 'shot'), may hold values from 0 to 127
- ray_table: int32 [2, 512], replicated, may hold values from -16 to 15
- receiver_grid: int32 [2, 1024], replicated, may hold values from 0 to 63
Outputs:
- encoded: bfloat16 [512, 16, 2, 1024], P(('shot', 'rcv'))
The draws below stay inside these ranges and needn't reach their ends.
All inputs are finite; a program needn't handle non-finite values.
Results may differ from the reference program's by a relative error of at most 0.0042.
Values may be sent and summed in bfloat16 or wider, within the bound.
No kernel may reach another device: no remote copies, remote signals or barrier semaphores. Data moves between devices by JAX's collectives and lax.ppermute only.
A program may use at most 64 MiB of HBM per device.

```python
import math
import jax
import jax.numpy as jnp
from jax import lax

FREQS = 16
RECEIVERS = 1024
RAYS = 512
SHOTS = 16384


def set_ends(values, rng, least, top_value):
    shape = values.shape
    index_at = [jax.random.randint(jax.random.fold_in(rng, axis), (), 0, shape[axis]) for axis in range(len(shape))]
    values = values.at[tuple(index_at)].set(least)
    longest = shape.index(max(shape))
    index_at[longest] = (index_at[longest] + 1) % shape[longest]
    return values.at[tuple(index_at)].set(top_value)


def block_scale(rng, shape, cuts, low, largest):
    def one(position, parts):
        steps = jax.random.uniform(jax.random.fold_in(jax.random.fold_in(rng, 6), position), (parts,), jnp.float32, low / len(cuts), largest / len(cuts))
        return jnp.repeat(jnp.exp(steps), shape[position] // parts).reshape((-1,) + (1,) * (len(shape) - position - 1))

    level = one(*cuts[0])
    for cut in cuts[1:]:
        level = level * one(*cut)
    return level


def normal_values(rng, shape, width, reach, cuts=(), held_as=jnp.bfloat16):
    values = jax.random.normal(rng, shape, jnp.float32) * width
    if len(cuts) > 0:
        values = block_scale(rng, shape, cuts, -0.22, 0.18) * values
    return jnp.clip(values, min=-reach, max=reach).astype(held_as)


def setup_inputs(seed: int = 0) -> dict:
    arg_keys = jax.random.split(jax.random.key(seed), 5)
    spectra = normal_values(arg_keys[0], (FREQS, SHOTS, 2, RECEIVERS), 1.0, 6.0, ((0, 16), (1, 16)))
    shot_grid = set_ends(jax.random.randint(arg_keys[1], (2, SHOTS), 0, 128), jax.random.fold_in(arg_keys[1], 1), 0, 127).astype(jnp.int32)
    ray_table = set_ends(jax.random.randint(arg_keys[2], (2, RAYS), -16, 16), jax.random.fold_in(arg_keys[2], 1), -16, 15).astype(jnp.int32)
    receiver_grid = set_ends(jax.random.randint(arg_keys[3], (2, RECEIVERS), 0, 64), jax.random.fold_in(arg_keys[3], 1), 0, 63).astype(jnp.int32)
    return {"spectra": spectra, "shot_grid": shot_grid, "ray_table": ray_table, "receiver_grid": receiver_grid}


base_index = 5
modulus = 1024

def reference(spectra, shot_grid, ray_table, receiver_grid):
    gscale = 1.0 / math.sqrt(SHOTS)
    step_angle = 2.0 * math.pi / modulus

    def one_frequency(findex):
        wave = base_index + findex
        shot_count = wave * (ray_table[0][:, None] * shot_grid[0][None, :] + ray_table[1][:, None] * shot_grid[1][None, :]) % modulus
        shot_angle = shot_count.astype(jnp.float32) * step_angle
        phases = jnp.concatenate([jnp.cos(shot_angle), jnp.sin(shot_angle)], 0).astype(jnp.bfloat16)
        block = lax.dynamic_index_in_dim(spectra, findex, 0, keepdims=False).reshape(SHOTS, 2 * RECEIVERS)
        product = jnp.dot(phases, block, preferred_element_type=jnp.float32)
        real_part = product[:RAYS, :RECEIVERS] + product[RAYS:, RECEIVERS:]
        imag_part = product[:RAYS, RECEIVERS:] - product[RAYS:, :RECEIVERS]
        rcv_count = wave * (ray_table[0][:, None] * receiver_grid[0][None, :] + ray_table[1][:, None] * receiver_grid[1][None, :]) % modulus
        rcv_angle = rcv_count.astype(jnp.float32) * step_angle
        cosine = jnp.cos(rcv_angle)
        sine = jnp.sin(rcv_angle)
        out_real = gscale * (real_part * cosine - imag_part * sine)
        out_imag = gscale * (real_part * sine + imag_part * cosine)
        return jnp.stack([out_real, out_imag], 1).astype(jnp.bfloat16)
    result = lax.map(one_frequency, jnp.arange(FREQS, dtype=jnp.int32))
    return jnp.transpose(result, (1, 0, 2, 3))
```

```python
import functools
import math

import jax
import jax.numpy as jnp
import numpy as np
from jax import lax
from jax.experimental import pallas as pl
from jax.experimental.pallas import tpu as pltpu
from jax.sharding import PartitionSpec as P

BASE = 5
MODULUS = 1024
ZH, XS, ZL, YS, CORES = 4, 4, 2, 4, 2
SHOT, RCV = ZH * XS, ZL * YS * CORES
RAYS, WIDTH, LOCAL = 512, 1024, 1024
SHARE = RAYS // SHOT
XFIRST = 24
ZFIRST = SHARE - XFIRST
VMEM = pl.BlockSpec(memory_space=pltpu.VMEM)
SMEM = pl.BlockSpec(memory_space=pltpu.SMEM)
ANY = pl.BlockSpec(memory_space=pl.ANY)


def fitted(fn, degree):
    points = 0.125 * (1 + np.cos(np.pi * (np.arange(400) + 0.5) / 400))
    series = np.polynomial.chebyshev.Chebyshev.fit(points, fn(np.sqrt(points)), degree, domain=[0, 0.25])
    return [float(a) for a in series.convert(kind=np.polynomial.Polynomial).coef]


COS = fitted(lambda f: np.cos(2 * np.pi * f), 5)
SIN = fitted(lambda f: np.sin(2 * np.pi * f) / f, 5)


def horner(coefs, v):
    total = v * coefs[-1] + coefs[-2]
    for a in coefs[-3::-1]:
        total = total * v + a
    return total


def cos_sin(turns):
    f = turns - jnp.round(turns)
    v = f * f
    return horner(COS, v), f * horner(SIN, v)


def place(index):
    shot, rcv = index // RCV, index % RCV
    return shot // XS, shot % XS, rcv // (YS * CORES), rcv // CORES % YS, rcv % CORES


def joined(zh, x, zl, y, core):
    return ((zh % ZH) * XS + x % XS) * RCV + (zl * YS + y) * CORES + core


def pairs(axis, steps):
    out = []
    for index in range(SHOT * RCV):
        zh, x, zl, y, core = place(index)
        step = steps[core]
        out.append((index, joined(zh + step, x, zl, y, core) if axis == "z" else joined(zh, x + step, zl, y, core)))
    return out


def send(value, axis, steps):
    return lax.ppermute(value, ("shot", "rcv"), pairs(axis, steps))


STEPS = ((2, 2), (1, 3), (3, 1))


def picked(ray, row_of_lane, rows):
    chosen = (lax.broadcasted_iota(jnp.int32, (rows, ray.shape[1]), 0) == row_of_lane).astype(jnp.bfloat16)
    return lax.dot_general(chosen, ray, (((1,), (1,)), ((), ())), preferred_element_type=jnp.float32)


def phase_rows(groups, info_ref, ray_ref, shot_ref, lhs):
    ray = ray_ref[...].astype(jnp.float32).astype(jnp.bfloat16)
    lane = lax.broadcasted_iota(jnp.int32, (1, RAYS), 1)
    zh_of, x_of, q_of = lane // (RAYS // ZH), lane // SHARE % XS, lane % SHARE
    odd = (lax.broadcasted_iota(jnp.int32, (1, 256), 1) % 2).astype(jnp.float32) * 0.25
    base = 0
    for slot, (axis, low, m) in enumerate(groups):
        target = info_ref[slot]
        along, other = (x_of, zh_of) if axis == "x" else (zh_of, x_of)
        mine = (along == target) & (q_of >= low) & (q_of < low + m)
        p = picked(ray, jnp.where(mine, other * m + q_of - low, -1), 4 * m)

        def step(k, carry, p=p, base=base, m=m):
            at = pl.ds(pl.multiple_of(k * 256, 256), 256)
            g0, g1 = shot_ref[0:1, at], shot_ref[1:2, at]
            for i in range(4):
                rays = p[i * m : (i + 1) * m]
                c, s = cos_sin(rays[:, 0:1] * g0 + rays[:, 1:2] * g1 - odd)
                lhs[base + 2 * m * i : base + 2 * m * (i + 1), at] = jnp.concatenate([c, -s], 0).astype(jnp.bfloat16)
            return carry

        lax.fori_loop(0, 2 * LOCAL // 256, step, 0)
        base += 8 * m


def products(groups, lhs, data_ref, outs):
    for i in range(WIDTH // 256):
        at = slice(i * 256, (i + 1) * 256)
        block = data_ref[:, at]
        base = 0
        for (axis, low, m), out in zip(groups, outs):
            r = jnp.dot(lhs[base : base + 8 * m], block, preferred_element_type=jnp.float32)
            out[:, at] = r.astype(out.dtype)
            base += 8 * m


def first_kernel(groups, info_ref, ray_ref, shot_ref, x_ref, *refs):
    outs, (data_ref, lhs, buf, sems) = refs[: len(groups)], refs[len(groups) :]
    part = LOCAL // 8
    copies = []
    for i in range(8):
        at = pl.ds(i * part, part)
        copies.append(pltpu.make_async_copy(x_ref.at[at], buf.at[at], sems.at[i]))
        copies[-1].start()
    phase_rows(groups, info_ref, ray_ref, shot_ref, lhs)
    for i in range(8):
        copies[i].wait()
        for s in range(i * part, (i + 1) * part, 8):
            data_ref[2 * s : 2 * s + 16] = buf[s : s + 8].reshape(16, WIDTH)
    products(groups, lhs, data_ref, outs)


def later_kernel(groups, info_ref, ray_ref, shot_ref, data_ref, *refs):
    outs, (lhs,) = refs[: len(groups)], refs[len(groups) :]
    phase_rows(groups, info_ref, ray_ref, shot_ref, lhs)
    products(groups, lhs, data_ref, outs)


def encode(groups, info, ray_table, shots, x, dtype, first):
    rows = sum(8 * m for _, _, m in groups)
    shapes = [jax.ShapeDtypeStruct((8 * m, WIDTH), dtype) for _, _, m in groups]
    scratch = [pltpu.VMEM((rows, 2 * LOCAL), jnp.bfloat16)]
    if first:
        shapes.append(jax.ShapeDtypeStruct((2 * LOCAL, WIDTH), jnp.bfloat16))
        scratch += [pltpu.VMEM((LOCAL, 2, WIDTH), jnp.bfloat16), pltpu.SemaphoreType.DMA((8,))]
    return pl.pallas_call(
        functools.partial(first_kernel if first else later_kernel, groups),
        out_shape=shapes,
        in_specs=[SMEM, VMEM, VMEM, ANY if first else VMEM],
        out_specs=[VMEM] * len(shapes),
        scratch_shapes=scratch,
        compiler_params=pltpu.CompilerParams(vmem_limit_bytes=28 * 2**20),
        cost_estimate=pl.CostEstimate(flops=2 * rows * 2 * LOCAL * WIDTH, bytes_accessed=8 * 2**20, transcendentals=0),
        name="encode_first" if first else "encode_later",
    )(info, ray_table, shots, x)


def merge_kernel(n_in, unit, info_ref, *refs):
    ins, outs = refs[:n_in], refs[n_in:]
    for k, out in enumerate(outs):
        at = pl.ds(pl.multiple_of(info_ref[k] * unit, 16), unit)
        total = ins[0][at, :].astype(jnp.float32)
        for piece in ins[1:]:
            total = total + piece[at, :].astype(jnp.float32)
        out[...] = total.astype(out.dtype)


def merge(info, own, received):
    unit = own.shape[0] // 4
    ins = [own, *received]
    return pl.pallas_call(
        functools.partial(merge_kernel, len(ins), unit),
        out_shape=[jax.ShapeDtypeStruct((unit, WIDTH), d) for d in (jnp.bfloat16,) * 3 + (jnp.float32,)],
        in_specs=[SMEM] + [VMEM] * len(ins),
        out_specs=[VMEM] * 4,
        name="merge",
    )(info, *ins)


def last_kernel(scale, info_ref, ray_ref, rcv_ref, *refs):
    ins, out = refs[:-1], refs[-1]
    target, turn = info_ref[0], info_ref[1].astype(jnp.float32) / MODULUS
    ray = ray_ref[...].astype(jnp.float32).astype(jnp.bfloat16)
    lane = lax.broadcasted_iota(jnp.int32, (1, RAYS), 1)
    p = picked(ray, lane - target * SHARE, SHARE)
    for i in range(WIDTH // 256):
        at = slice(i * 256, (i + 1) * 256)
        grid = rcv_ref[:, at].astype(jnp.float32)
        c, s = cos_sin((p[:, 0:1] * grid[0:1] + p[:, 1:2] * grid[1:2]) * turn)
        parts = []
        for some in (ins[:4], ins[4:]):
            total = some[0][:, at]
            for piece in some[1:]:
                total = total + piece[:, at].astype(jnp.float32)
            parts.append(total)
        re = jnp.concatenate([parts[0][:XFIRST], parts[1][:ZFIRST]], 0)
        im = jnp.concatenate([parts[0][XFIRST:], parts[1][ZFIRST:]], 0)
        out[0, :, at] = (scale * (re * c - im * s)).astype(jnp.bfloat16)
        out[1, :, at] = (scale * (re * s + im * c)).astype(jnp.bfloat16)


def on_device(spectra, shot_grid, ray_table, receiver_grid):
    shot, rcv = lax.axis_index("shot"), lax.axis_index("rcv")
    zh, x, core = shot // XS, shot % XS, rcv % CORES
    wave = BASE + rcv
    scale = 1.0 / math.sqrt(LOCAL * SHOT)
    shots = jnp.repeat(shot_grid, 2, axis=1).astype(jnp.float32) * (wave.astype(jnp.float32) / MODULUS)

    def goal(at, steps):
        return (at + jnp.where(core == 0, steps[0], steps[1])) % 4

    xs = [goal(x, s) for s in STEPS] + [x]
    zs = [goal(zh, s) for s in STEPS] + [zh]
    px, qz = ("x", 0, XFIRST), ("z", XFIRST, ZFIRST)
    data = spectra.reshape(LOCAL, 2, WIDTH)

    def info(*values):
        return jnp.stack([v.astype(jnp.int32) for v in values])

    p0, q0, data = encode([px, qz], info(xs[0], zs[0]), ray_table, shots, data, jnp.bfloat16, True)
    from_x = [send(p0, "x", STEPS[0])]
    from_z = [send(q0, "z", STEPS[0])]
    p1, p2, q1, q2 = encode([px, px, qz, qz], info(xs[1], xs[2], zs[1], zs[2]), ray_table, shots, data, jnp.bfloat16, False)
    from_x += [send(p1, "x", STEPS[1]), send(p2, "x", STEPS[2])]
    from_z += [send(q1, "z", STEPS[1]), send(q2, "z", STEPS[2])]
    p3, q3 = encode([px, qz], info(xs[3], zs[3]), ray_table, shots, data, jnp.float32, False)
    half = merge(info(*zs), p3, from_x)
    other = merge(info(*xs), q3, from_z)
    ins = [half[3]] + [send(half[k], "z", STEPS[k]) for k in range(3)]
    ins += [other[3]] + [send(other[k], "x", STEPS[k]) for k in range(3)]
    turned = pl.pallas_call(
        functools.partial(last_kernel, scale),
        out_shape=jax.ShapeDtypeStruct((2, SHARE, WIDTH), jnp.bfloat16),
        in_specs=[SMEM] + [VMEM] * 10,
        out_specs=VMEM,
        name="last",
    )(info(shot, wave), ray_table, receiver_grid, *ins)
    mine = jnp.transpose(turned, (1, 0, 2)).reshape(SHARE, 1, 2, WIDTH)
    return lax.all_to_all(mine, "rcv", split_axis=0, concat_axis=1, tiled=True)


def solution(mesh):
    in_specs = (P("rcv", "shot", None, None), P(None, "shot"), P(), P())
    out_specs = P(("shot", "rcv"), None, None, None)
    return jax.shard_map(on_device, mesh=mesh, in_specs=in_specs, out_specs=out_specs, check_vma=False)
```

```python
import functools
import math

import jax
import jax.numpy as jnp
import numpy as np
from jax import lax
from jax.experimental import pallas as pl
from jax.experimental.pallas import tpu as pltpu
from jax.sharding import PartitionSpec as P

BASE = 5
MODULUS = 1024
ZH, XS, ZL, YS, CORES = 4, 4, 2, 4, 2
SHOT, RCV = ZH * XS, ZL * YS * CORES
RAYS, WIDTH, LOCAL = 512, 1024, 1024
SHARE = RAYS // SHOT
XFIRST = 24
ZFIRST = SHARE - XFIRST
VMEM = pl.BlockSpec(memory_space=pltpu.VMEM)
SMEM = pl.BlockSpec(memory_space=pltpu.SMEM)
STEPS = ((2, 2), (1, 3), (3, 1), (0, 0))
F32, BF16 = jnp.float32, jnp.bfloat16


def fitted(fn, degree):
    points = 0.125 * (1 + np.cos(np.pi * (np.arange(400) + 0.5) / 400))
    series = np.polynomial.chebyshev.Chebyshev.fit(points, fn(np.sqrt(points)), degree, domain=[0, 0.25])
    return [float(a) for a in series.convert(kind=np.polynomial.Polynomial).coef]


HALF_COS = fitted(lambda f: np.cos(np.pi * f), 4)
HALF_SIN = fitted(lambda f: np.sin(np.pi * f) / f, 3)


def horner(coefs, v):
    total = v * coefs[-1] + coefs[-2]
    for a in coefs[-3::-1]:
        total = total * v + a
    return total


def cos_minus_sin(turns):
    f = turns - jnp.round(turns)
    v = f * f
    s = f * horner(HALF_SIN, v)
    twice = s * -2.0
    return twice * s + 1.0, twice * horner(HALF_COS, v)


def iota(shape, axis):
    return lax.broadcasted_iota(jnp.int32, shape, axis)


def position(ref):
    return ref[0], ref[1], ref[2], ref[3]


def goal(at, core, step):
    return (at + jnp.where(core == 0, step[0], step[1])) % 4


def ray_columns(ray_ref):
    row = iota((8, RAYS), 0)
    r0, r1 = ray_ref[0:1, :].astype(F32), ray_ref[1:2, :].astype(F32)
    return jnp.where(row < 2, r0, jnp.where(row < 4, r1, jnp.where(row == 4, 1.0, 0.0))).astype(BF16)


def picked(columns, row_of_lane, rows, wave):
    chosen = (iota((rows, RAYS), 0) == row_of_lane).astype(BF16)
    p = lax.dot_general(chosen, columns, (((1,), (1,)), ((), ())), preferred_element_type=F32)
    col = iota((rows, 8), 1)
    p = jnp.where(col < 4, p * (wave.astype(F32) / MODULUS), p)
    high = p.astype(BF16).astype(F32)
    return jnp.where((col == 1) | (col == 3), p - high, high).astype(BF16)


def grid_rows(grid_ref, shots_ref):
    row = iota((8, LOCAL), 0)
    g = jnp.where(row < 2, grid_ref[0:1, :], jnp.where(row < 4, grid_ref[1:2, :], 0)).astype(F32).astype(BF16)
    twice = (iota((128, 256), 0) == iota((128, 256), 1) // 2).astype(BF16)
    quarter = jnp.where(iota((8, 256), 0) == 4, (iota((8, 256), 1) % 2).astype(F32) * -0.25, 0.0)
    for i in range(LOCAL // 128):
        wide = jnp.dot(g[:, i * 128 : (i + 1) * 128], twice, preferred_element_type=F32) + quarter
        shots_ref[:, i * 256 : (i + 1) * 256] = wide.astype(BF16)


def phase_rows(group, where, columns, shots_ref, lhs, base, chunk=256):
    axis, low, m, step = group
    zh, x, core, wave = where
    lane = iota((1, RAYS), 1)
    zh_of, x_of, q_of = lane // (RAYS // ZH), lane // SHARE % XS, lane % SHARE
    along, other, at = (x_of, zh_of, x) if axis == "x" else (zh_of, x_of, zh)
    mine = (along == goal(at, core, step)) & (q_of >= low) & (q_of < low + m)
    p = picked(columns, jnp.where(mine, other * m + q_of - low, -1), 4 * m, wave)
    for k in range(0, 2 * LOCAL, chunk):
        c, s = cos_minus_sin(jnp.dot(p, shots_ref[:, k : k + chunk], preferred_element_type=F32))
        for i in range(4):
            unit = jnp.concatenate([c[i * m : (i + 1) * m], s[i * m : (i + 1) * m]], 0)
            lhs[base + 2 * m * i : base + 2 * m * (i + 1), k : k + chunk] = unit.astype(BF16)


def products(rows, lhs, base, data_ref, out):
    for i in range(0, WIDTH, 256):
        r = jnp.dot(lhs[base : base + rows], data_ref[:, i : i + 256], preferred_element_type=F32)
        out[:, i : i + 256] = r.astype(out.dtype)


def first_kernel(groups, place_ref, ray_ref, grid_ref, x_ref, *refs):
    outs, (data_ref, shots_ref, lhs, buf, ray_buf, grid_buf, sems) = refs[: len(groups)], refs[len(groups) :]
    small = [pltpu.make_async_copy(ray_ref, ray_buf, sems.at[8]), pltpu.make_async_copy(grid_ref, grid_buf, sems.at[9])]
    for copy in small:
        copy.start()
    part = LOCAL // 8
    copies = []
    for i in range(8):
        at = pl.ds(i * part, part)
        copies.append(pltpu.make_async_copy(x_ref.at[at], buf.at[at], sems.at[i]))
        copies[-1].start()
    for copy in small:
        copy.wait()
    where = position(place_ref)
    columns = ray_columns(ray_buf)
    grid_rows(grid_buf, shots_ref)
    base = 0
    for group in groups:
        phase_rows(group, where, columns, shots_ref, lhs, base)
        base += 8 * group[2]
    for i in range(8):
        copies[i].wait()
        for s in range(i * part, (i + 1) * part, 8):
            data_ref[2 * s : 2 * s + 16] = buf[s : s + 8].reshape(16, WIDTH)
    base = 0
    for group, out in zip(groups, outs):
        products(8 * group[2], lhs, base, data_ref, out)
        base += 8 * group[2]


def later_kernel(groups, place_ref, ray_ref, shots_ref, data_ref, *refs):
    outs, (lhs,) = refs[: len(groups)], refs[len(groups) :]
    where = position(place_ref)
    columns = ray_columns(ray_ref)
    base = 0
    for group, out in zip(groups, outs):
        phase_rows(group, where, columns, shots_ref, lhs, base)
        products(8 * group[2], lhs, base, data_ref, out)
        base += 8 * group[2]


def encode(groups, spot, ray_table, shots, x, dtype, first):
    rows = sum(8 * g[2] for g in groups)
    shapes = [jax.ShapeDtypeStruct((8 * g[2], WIDTH), dtype) for g in groups]
    scratch = [pltpu.VMEM((rows, 2 * LOCAL), BF16)]
    if first:
        shapes += [jax.ShapeDtypeStruct((2 * LOCAL, WIDTH), BF16), jax.ShapeDtypeStruct((8, 2 * LOCAL), BF16)]
        scratch += [pltpu.VMEM((LOCAL, 2, WIDTH), BF16), pltpu.VMEM((2, RAYS), jnp.int32), pltpu.VMEM((2, LOCAL), jnp.int32)]
        scratch += [pltpu.SemaphoreType.DMA((10,))]
    if first:
        ray_table, shots, x = (pltpu.with_memory_space_constraint(a, pltpu.HBM) for a in (ray_table, shots, x))
    return pl.pallas_call(
        functools.partial(first_kernel if first else later_kernel, groups),
        out_shape=shapes,
        in_specs=[SMEM] + ([pl.BlockSpec(memory_space=pltpu.HBM)] * 3 if first else [VMEM] * 3),
        out_specs=[VMEM] * len(shapes),
        scratch_shapes=scratch,
        compiler_params=pltpu.CompilerParams(vmem_limit_bytes=20 * 2**20),
        cost_estimate=pl.CostEstimate(flops=2 * rows * 2 * LOCAL * WIDTH, bytes_accessed=8 * 2**20, transcendentals=0),
        name="encode_first" if first else "encode_later",
    )(spot, ray_table, shots, x)


def place(index):
    shot, rcv = index // RCV, index % RCV
    return shot // XS, shot % XS, rcv // (YS * CORES), rcv // CORES % YS, rcv % CORES


def joined(zh, x, zl, y, core):
    return ((zh % ZH) * XS + x % XS) * RCV + (zl * YS + y) * CORES + core


def send(value, axis, steps):
    pairs = []
    for index in range(SHOT * RCV):
        zh, x, zl, y, core = place(index)
        step = steps[core]
        pairs.append((index, joined(zh + step, x, zl, y, core) if axis == "z" else joined(zh, x + step, zl, y, core)))
    return lax.ppermute(value, ("shot", "rcv"), pairs)


def merge_kernel(axis, place_ref, own, *refs):
    ins, outs = refs[:3], refs[3:]
    zh, x, core, _ = position(place_ref)
    unit = own.shape[0] // 4
    for step, out in zip(STEPS, outs):
        at = pl.ds(pl.multiple_of(goal(zh if axis == "x" else x, core, step) * unit, 16), unit)
        total = own[at, :]
        for piece in ins:
            total = total + piece[at, :].astype(F32)
        out[...] = total.astype(out.dtype)


def merge(axis, spot, own, received):
    unit = own.shape[0] // 4
    return pl.pallas_call(
        functools.partial(merge_kernel, axis),
        out_shape=[jax.ShapeDtypeStruct((unit, WIDTH), d) for d in (BF16, BF16, BF16, F32)],
        in_specs=[SMEM] + [VMEM] * 4,
        out_specs=[VMEM] * 4,
        compiler_params=pltpu.CompilerParams(vmem_limit_bytes=12 * 2**20),
        name="merge_" + axis,
    )(spot, own, *received)


def last_kernel(scale, place_ref, ray_ref, rcv_ref, *refs):
    ins, (out, rows) = refs[:8], refs[8:]
    zh, x, core, wave = position(place_ref)
    shot = zh * XS + x
    row = iota((8, WIDTH), 0)
    grid = jnp.where(row < 2, rcv_ref[0:1, :], jnp.where(row < 4, rcv_ref[1:2, :], 0)).astype(F32).astype(BF16)
    p = picked(ray_columns(ray_ref), iota((1, RAYS), 1) - shot * SHARE, SHARE, wave)
    for i in range(0, WIDTH, 256):
        at = slice(i, i + 256)
        c, s = cos_minus_sin(jnp.dot(p, grid[:, at], preferred_element_type=F32))
        parts = []
        for some in (ins[:4], ins[4:]):
            total = some[0][:, at]
            for piece in some[1:]:
                total = total + piece[:, at].astype(F32)
            parts.append(total)
        re = jnp.concatenate([parts[0][:XFIRST], parts[1][:ZFIRST]], 0)
        im = jnp.concatenate([parts[0][XFIRST:], parts[1][ZFIRST:]], 0)
        turned = (scale * (re * c + im * s), scale * (im * c - re * s))
        for k in range(2):
            for j in range(i, i + 256, 128):
                rows[j // 128, pl.ds(k, SHARE, stride=2), :] = turned[k][:, j - i : j - i + 128]
        for j in range(i, i + 256, 128):
            out[:, j : j + 128] = rows[j // 128].astype(BF16)


def last(scale, spot, ray_table, receiver_grid, ins):
    return pl.pallas_call(
        functools.partial(last_kernel, scale),
        out_shape=jax.ShapeDtypeStruct((2 * SHARE, WIDTH), BF16),
        in_specs=[SMEM] + [VMEM] * 10,
        out_specs=VMEM,
        scratch_shapes=[pltpu.VMEM((WIDTH // 128, 2 * SHARE, 128), F32)],
        compiler_params=pltpu.CompilerParams(vmem_limit_bytes=8 * 2**20),
        name="last",
    )(spot, ray_table, receiver_grid, *ins)


def on_device(spectra, shot_grid, ray_table, receiver_grid):
    scale = 1.0 / math.sqrt(LOCAL * SHOT)
    shot, rcv = lax.axis_index("shot"), lax.axis_index("rcv")
    spot = jnp.stack([shot // XS, shot % XS, rcv % CORES, BASE + rcv]).astype(jnp.int32)
    px, qz = ("x", 0, XFIRST), ("z", XFIRST, ZFIRST)
    groups = [[px + (s,) for s in STEPS], [qz + (s,) for s in STEPS]]
    p0, q0, data, shots = encode([g[0] for g in groups], spot, ray_table, shot_grid, spectra.reshape(LOCAL, 2, WIDTH), BF16, True)
    from_x, from_z = [send(p0, "x", STEPS[0])], [send(q0, "z", STEPS[0])]
    p1, p2, q1, q2 = encode(groups[0][1:3] + groups[1][1:3], spot, ray_table, shots, data, BF16, False)
    from_x += [send(p1, "x", STEPS[1]), send(p2, "x", STEPS[2])]
    from_z += [send(q1, "z", STEPS[1]), send(q2, "z", STEPS[2])]
    shots, p1 = lax.optimization_barrier((shots, p1))
    p3, q3 = encode([g[3] for g in groups], spot, ray_table, shots, data, F32, False)
    half = merge("x", spot, p3, from_x)
    other = merge("z", spot, q3, from_z)
    ins = [half[3]] + [send(half[k], "z", STEPS[k]) for k in range(3)]
    ins += [other[3]] + [send(other[k], "x", STEPS[k]) for k in range(3)]
    turned = last(scale, spot, ray_table, receiver_grid, ins)
    return lax.all_to_all(turned.reshape(SHARE, 1, 2, WIDTH), "rcv", split_axis=0, concat_axis=1, tiled=True)


def solution(mesh):
    in_specs = (P("rcv", "shot", None, None), P(None, "shot"), P(), P())
    out_specs = P(("shot", "rcv"), None, None, None)
    return jax.shard_map(on_device, mesh=mesh, in_specs=in_specs, out_specs=out_specs, check_vma=False)
```

```python
import functools
import math

import jax
import jax.numpy as jnp
import numpy as np
from jax import lax
from jax.experimental import pallas as pl
from jax.experimental.pallas import tpu as pltpu
from jax.sharding import Mesh
from jax.sharding import PartitionSpec as P

BASE = 5
MODULUS = 1024
ZH, XS, RCV, CORES = 4, 4, 16, 2
RAYS, WIDTH, LOCAL = 512, 1024, 1024
SHARE = RAYS // (ZH * XS)
ROWS = 2 * ZH * SHARE
DEPTH = 2 * LOCAL
VMEM = pl.BlockSpec(memory_space=pltpu.VMEM)
SMEM = pl.BlockSpec(memory_space=pltpu.SMEM)
HBM = pl.BlockSpec(memory_space=pltpu.HBM)
FAR, NEAR, BACK, HERE = (2, 0), (0, 1), (0, -1), (0, 0)
F32, BF16 = jnp.float32, jnp.bfloat16


def fitted(fn, degree):
    points = 0.125 * (1 + np.cos(np.pi * (np.arange(400) + 0.5) / 400))
    series = np.polynomial.chebyshev.Chebyshev.fit(points, fn(np.sqrt(points)), degree, domain=[0, 0.25])
    return [float(a) for a in series.convert(kind=np.polynomial.Polynomial).coef]


HALF_COS = fitted(lambda f: np.cos(np.pi * f), 4)
HALF_SIN = fitted(lambda f: np.sin(np.pi * f) / f, 4)
ROOT_SIN = fitted(lambda f: math.sqrt(2.0) * np.sin(np.pi * f) / f, 4)


def horner(coefs, v):
    total = v * coefs[-1] + coefs[-2]
    for a in coefs[-3::-1]:
        total = total * v + a
    return total


def cosine(turns):
    f = turns - jnp.round(turns)
    t = f * horner(ROOT_SIN, f * f)
    return 1.0 - t * t


def cos_minus_sin(turns):
    f = turns - jnp.round(turns)
    v = f * f
    s = f * horner(HALF_SIN, v)
    twice = s * -2.0
    return twice * s + 1.0, twice * horner(HALF_COS, v)


def iota(shape, axis):
    return lax.broadcasted_iota(jnp.int32, shape, axis)


def ray_columns(ray_ref):
    row = iota((8, RAYS), 0)
    r0, r1 = ray_ref[0:1, :].astype(F32), ray_ref[1:2, :].astype(F32)
    return jnp.where(row < 2, r0, jnp.where(row < 4, r1, jnp.where(row == 4, 1.0, 0.0))).astype(BF16)


def picked(columns, lane_of_row, turn, quarters):
    rows = lane_of_row.shape[0]
    chosen = (iota((rows, RAYS), 1) == lane_of_row).astype(BF16)
    p = lax.dot_general(chosen, columns, (((1,), (1,)), ((), ())), preferred_element_type=F32)
    col = iota((rows, 8), 1)
    p = jnp.where(col < 4, p * turn, p)
    high = p.astype(BF16).astype(F32)
    p = jnp.where((col == 1) | (col == 3), p - high, high)
    return jnp.where(col == 5, quarters, p).astype(BF16)


def grid_rows(grid_ref, shots_ref):
    row = iota((8, LOCAL), 0)
    g = jnp.where(row < 2, grid_ref[0:1, :], jnp.where(row < 4, grid_ref[1:2, :], 0)).astype(F32).astype(BF16)
    twice = (iota((128, 256), 0) == iota((128, 256), 1) // 2).astype(BF16)
    rest = iota((8, 256), 0)
    rest = jnp.where(rest == 4, (iota((8, 256), 1) % 2).astype(F32) * -0.25, jnp.where(rest == 5, 1.0, 0.0))
    for i in range(LOCAL // 128):
        wide = jnp.dot(g[:, i * 128 : (i + 1) * 128], twice, preferred_element_type=F32) + rest
        shots_ref[:, i * 256 : (i + 1) * 256] = wide.astype(BF16)


def chosen_rows(step, place_ref, columns):
    here, wave, turn, first_stride, other_stride = (place_ref[k] for k in (2, 3, 4, 5, 6))
    target = (here + step[0] + step[1] * turn) % 4
    row = iota((ROWS, 1), 0)
    lane = row // (2 * SHARE) * other_stride + target * first_stride + row // 2 % SHARE
    quarters = (row % 2).astype(F32) * 0.25
    return picked(columns, lane, wave.astype(F32) / MODULUS, quarters)


def phase_rows(p, shots_ref, lhs, start, stop):
    for k in range(start, stop, 256):
        lhs[:, k : k + 256] = cosine(jnp.dot(p, shots_ref[:, k : k + 256], preferred_element_type=F32)).astype(BF16)


def first_kernel(place_ref, ray_ref, grid_ref, x_ref, out, data_ref, shots_ref, lhs, total, buf, ray_buf, grid_buf, sems):
    small = [pltpu.make_async_copy(ray_ref, ray_buf, sems.at[8]), pltpu.make_async_copy(grid_ref, grid_buf, sems.at[9])]
    for copy in small:
        copy.start()
    part = LOCAL // 8
    copies = []
    for i in range(8):
        at = pl.ds(i * part, part)
        copies.append(pltpu.make_async_copy(x_ref.at[at], buf.at[at], sems.at[i]))
        copies[-1].start()
    for copy in small:
        copy.wait()
    grid_rows(grid_buf, shots_ref)
    p = chosen_rows(FAR, place_ref, ray_columns(ray_buf))
    phase_rows(p, shots_ref, lhs, 0, DEPTH)
    for i in range(0, 8, 2):
        copies[i].wait()
        copies[i + 1].wait()
        for s in range(i * part, (i + 2) * part, 8):
            data_ref[2 * s : 2 * s + 16] = buf[s : s + 8].reshape(16, WIDTH)
        depth = slice(2 * i * part, 2 * (i + 2) * part)
        for n in range(0, WIDTH, 256):
            r = jnp.dot(lhs[:, depth], data_ref[depth, n : n + 256], preferred_element_type=F32)
            if i > 0:
                r = r + total[:, n : n + 256]
            if i < 6:
                total[:, n : n + 256] = r
            else:
                out[:, n : n + 256] = r.astype(out.dtype)


def first(spot, ray_table, shot_grid, data):
    held = [pltpu.with_memory_space_constraint(a, pltpu.HBM) for a in (ray_table, shot_grid, data)]
    return pl.pallas_call(
        first_kernel,
        out_shape=[jax.ShapeDtypeStruct((n, m), BF16) for n, m in ((ROWS, WIDTH), (DEPTH, WIDTH), (8, DEPTH))],
        in_specs=[SMEM, HBM, HBM, HBM],
        out_specs=[VMEM] * 3,
        scratch_shapes=[
            pltpu.VMEM((ROWS, DEPTH), BF16),
            pltpu.VMEM((ROWS, WIDTH), F32),
            pltpu.VMEM((LOCAL, 2, WIDTH), BF16),
            pltpu.VMEM((2, RAYS), jnp.int32),
            pltpu.VMEM((2, LOCAL), jnp.int32),
            pltpu.SemaphoreType.DMA((10,)),
        ],
        compiler_params=pltpu.CompilerParams(vmem_limit_bytes=20 * 2**20),
        cost_estimate=pl.CostEstimate(flops=2 * ROWS * DEPTH * WIDTH, bytes_accessed=8 * 2**20, transcendentals=0),
        name="encode_first",
    )(spot, *held)


def later_kernel(steps, place_ref, ray_ref, shots_ref, data_ref, *refs):
    outs, lhs = refs[: len(steps)], refs[len(steps) :]
    columns = ray_columns(ray_ref)
    ps = [chosen_rows(step, place_ref, columns) for step in steps]
    phase_rows(ps[0], shots_ref, lhs[0], 0, DEPTH)
    for i, out in enumerate(outs):
        for n in range(4):
            if i + 1 < len(outs):
                phase_rows(ps[i + 1], shots_ref, lhs[i + 1], n * DEPTH // 4, (n + 1) * DEPTH // 4)
            at = slice(n * 256, (n + 1) * 256)
            out[:, at] = jnp.dot(lhs[i][...], data_ref[:, at], preferred_element_type=F32).astype(out.dtype)


def later(steps, dtypes, spot, ray_table, shots, data):
    return pl.pallas_call(
        functools.partial(later_kernel, steps),
        out_shape=[jax.ShapeDtypeStruct((ROWS, WIDTH), dtype) for dtype in dtypes],
        in_specs=[SMEM] + [VMEM] * 3,
        out_specs=[VMEM] * len(steps),
        scratch_shapes=[pltpu.VMEM((ROWS, DEPTH), BF16)] * len(steps),
        compiler_params=pltpu.CompilerParams(vmem_limit_bytes=20 * 2**20),
        cost_estimate=pl.CostEstimate(flops=2 * len(steps) * ROWS * DEPTH * WIDTH, bytes_accessed=8 * 2**20, transcendentals=0),
        name="encode_later",
    )(spot, ray_table, shots, data)


def add_kernel(own, *refs):
    total = own[...]
    for piece in refs[:-1]:
        total = total + piece[...].astype(F32)
    refs[-1][...] = total.astype(BF16)


def add(own, *pieces):
    return pl.pallas_call(
        add_kernel,
        out_shape=jax.ShapeDtypeStruct(own.shape, BF16),
        in_specs=[VMEM] * (1 + len(pieces)),
        out_specs=VMEM,
        compiler_params=pltpu.CompilerParams(vmem_limit_bytes=8 * 2**20),
        name="add",
    )(own, *pieces)


def spread_kernel(place_ref, own, back, near, *outs):
    there, turn = place_ref[7], place_ref[4]
    unit = own.shape[0] // 4
    for step, out in zip((FAR, NEAR, BACK, HERE), outs):
        target = (there + step[0] + step[1] * turn) % 4
        at = pl.ds(pl.multiple_of(target * unit, unit), unit)
        out[...] = (own[at, :] + back[at, :].astype(F32) + near[at, :].astype(F32)).astype(out.dtype)


def spread(spot, own, back, near):
    unit = own.shape[0] // 4
    return pl.pallas_call(
        spread_kernel,
        out_shape=[jax.ShapeDtypeStruct((unit, WIDTH), dtype) for dtype in (BF16, BF16, BF16, F32)],
        in_specs=[SMEM] + [VMEM] * 3,
        out_specs=[VMEM] * 4,
        compiler_params=pltpu.CompilerParams(vmem_limit_bytes=8 * 2**20),
        name="spread",
    )(spot, own, back, near)


def last_kernel(scale, place_ref, ray_ref, rcv_ref, own, far, near, back, out):
    zh, x, wave = place_ref[0], place_ref[1], place_ref[3]
    count = 2 * SHARE
    row8 = iota((8, WIDTH), 0)
    grid = jnp.where(row8 < 2, rcv_ref[0:1, :], jnp.where(row8 < 4, rcv_ref[1:2, :], 0)).astype(F32).astype(BF16)
    row = iota((count, 1), 0)
    lane = zh * (RAYS // ZH) + x * SHARE + row // 2
    p = picked(ray_columns(ray_ref), lane, wave.astype(F32) / MODULUS, 0.0)
    real = row % 2 == 0
    for i in range(0, WIDTH, 256):
        at = slice(i, i + 256)
        c, s = cos_minus_sin(jnp.dot(p, grid[:, at], preferred_element_type=F32))
        total = own[:, at] + far[:, at].astype(F32) + near[:, at].astype(F32) + back[:, at].astype(F32)
        crossed = jnp.where(real, pltpu.roll(total, count - 1, 0), -pltpu.roll(total, 1, 0))
        out[:, at] = (scale * (total * c + crossed * s)).astype(BF16)


def last(scale, spot, ray_table, receiver_grid, *pieces):
    return pl.pallas_call(
        functools.partial(last_kernel, scale),
        out_shape=jax.ShapeDtypeStruct((2 * SHARE, WIDTH), BF16),
        in_specs=[SMEM] + [VMEM] * 6,
        out_specs=VMEM,
        compiler_params=pltpu.CompilerParams(vmem_limit_bytes=8 * 2**20),
        name="last",
    )(spot, ray_table, receiver_grid, *pieces)


def send(value, leg, step):
    pairs = []
    for index in range(ZH * XS * RCV):
        zh, x, rcv = index // (XS * RCV), index // RCV % XS, index % RCV
        move = step[0] + step[1] * (1 - rcv // (RCV // 2) * 2)
        if (rcv % CORES == 0) == (leg == 0):
            x = (x + move) % XS
        else:
            zh = (zh + move) % ZH
        pairs.append((index, (zh * XS + x) * RCV + rcv))
    return lax.ppermute(value, ("z_hi", "x", "rcv"), pairs)


def on_device(spectra, shot_grid, ray_table, receiver_grid):
    scale = 1.0 / math.sqrt(LOCAL * ZH * XS)
    zh, x, rcv = (lax.axis_index(name) for name in ("z_hi", "x", "rcv"))
    first_x = rcv % CORES == 0
    turn = 1 - rcv // (RCV // 2) * 2
    along_x, along_z = SHARE, RAYS // ZH
    spot = [zh, x, jnp.where(first_x, x, zh), BASE + rcv, turn]
    spot += [jnp.where(first_x, along_x, along_z), jnp.where(first_x, along_z, along_x), jnp.where(first_x, zh, x)]
    spot = jnp.stack(spot).astype(jnp.int32)
    far, data, shots = first(spot, ray_table, shot_grid, spectra.reshape(LOCAL, 2, WIDTH))
    relayed = send(far, 0, NEAR)
    back, near = later([BACK, NEAR], [BF16, F32], spot, ray_table, shots, data)
    from_back = send(back, 0, BACK)
    from_near = send(add(near, relayed), 0, NEAR)
    shots, back = lax.optimization_barrier((shots, back))
    (here,) = later([HERE], [F32], spot, ray_table, shots, data)
    far, near, back, here = spread(spot, here, from_back, from_near)
    pieces = [send(far, 1, FAR), send(near, 1, NEAR), send(back, 1, BACK)]
    turned = last(scale, spot, ray_table, receiver_grid, here, *pieces)
    return lax.all_to_all(turned.reshape(SHARE, 1, 2, WIDTH), "rcv", split_axis=0, concat_axis=1, tiled=True)


def solution(mesh):
    split = Mesh(mesh.devices.reshape(ZH, XS, RCV), ("z_hi", "x", "rcv"))
    in_specs = (P("rcv", ("z_hi", "x"), None, None), P(None, ("z_hi", "x")), P(), P())
    out_specs = P(("z_hi", "x", "rcv"), None, None, None)
    return jax.shard_map(on_device, mesh=split, in_specs=in_specs, out_specs=out_specs, check_vma=False)
```

```python
import functools
import math

import jax
import jax.numpy as jnp
import numpy as np
from jax import lax
from jax.experimental import pallas as pl
from jax.experimental.pallas import tpu as pltpu
from jax.sharding import Mesh
from jax.sharding import PartitionSpec as P

BASE = 5
MODULUS = 1024
ZH, XS, RCV, CORES = 4, 4, 16, 2
RAYS, WIDTH, LOCAL = 512, 1024, 1024
SHARE = RAYS // (ZH * XS)
ROWS = 2 * ZH * SHARE
DEPTH = 2 * LOCAL
VMEM = pl.BlockSpec(memory_space=pltpu.VMEM)
SMEM = pl.BlockSpec(memory_space=pltpu.SMEM)
HBM = pl.BlockSpec(memory_space=pltpu.HBM)
FAR, NEAR, BACK, HERE = (2, 0), (0, 1), (0, -1), (0, 0)
SCALE = 1.0 / math.sqrt(LOCAL * ZH * XS)
F32, BF16 = jnp.float32, jnp.bfloat16


def fitted(fn, degree):
    points = 0.125 * (1 + np.cos(np.pi * (np.arange(400) + 0.5) / 400))
    series = np.polynomial.chebyshev.Chebyshev.fit(points, fn(np.sqrt(points)), degree, domain=[0, 0.25])
    return [float(a) for a in series.convert(kind=np.polynomial.Polynomial).coef]


HALF_COS = fitted(lambda f: np.cos(np.pi * f), 4)
HALF_SIN = fitted(lambda f: np.sin(np.pi * f) / f, 4)
ROOT_SIN = fitted(lambda f: math.sqrt(2.0) * np.sin(np.pi * f) / f, 4)


def horner(coefs, v):
    total = v * coefs[-1] + coefs[-2]
    for a in coefs[-3::-1]:
        total = total * v + a
    return total


def cosine(turns):
    f = turns - jnp.round(turns)
    t = f * horner(ROOT_SIN, f * f)
    return 1.0 - t * t


def cos_minus_sin(turns):
    f = turns - jnp.round(turns)
    v = f * f
    s = f * horner(HALF_SIN, v)
    twice = s * -2.0
    return twice * s + 1.0, twice * horner(HALF_COS, v)


def iota(shape, axis):
    return lax.broadcasted_iota(jnp.int32, shape, axis)


def ray_columns(ray_ref):
    row = iota((8, RAYS), 0)
    r0, r1 = ray_ref[0:1, :].astype(F32), ray_ref[1:2, :].astype(F32)
    return jnp.where(row < 2, r0, jnp.where(row < 4, r1, jnp.where(row == 4, 1.0, 0.0))).astype(BF16)


def picked(columns, lane_of_row, turn, quarters):
    rows = lane_of_row.shape[0]
    chosen = (iota((rows, RAYS), 1) == lane_of_row).astype(BF16)
    p = lax.dot_general(chosen, columns, (((1,), (1,)), ((), ())), preferred_element_type=F32)
    col = iota((rows, 8), 1)
    p = jnp.where(col < 4, p * turn, p)
    high = p.astype(BF16).astype(F32)
    p = jnp.where((col == 1) | (col == 3), p - high, high)
    return jnp.where(col == 5, quarters, p).astype(BF16)


def grid_rows(grid_ref, shots_ref):
    row = iota((8, LOCAL), 0)
    g = jnp.where(row < 2, grid_ref[0:1, :], jnp.where(row < 4, grid_ref[1:2, :], 0)).astype(F32).astype(BF16)
    twice = (iota((128, 256), 0) == iota((128, 256), 1) // 2).astype(BF16)
    rest = iota((8, 256), 0)
    rest = jnp.where(rest == 4, (iota((8, 256), 1) % 2).astype(F32) * -0.25, jnp.where(rest == 5, 1.0, 0.0))
    for i in range(LOCAL // 128):
        wide = jnp.dot(g[:, i * 128 : (i + 1) * 128], twice, preferred_element_type=F32) + rest
        shots_ref[:, i * 256 : (i + 1) * 256] = wide.astype(BF16)


def chosen_rows(step, place_ref, columns):
    here, wave, turn, first_stride, other_stride, there = (place_ref[k] for k in (2, 3, 4, 5, 6, 7))
    target = (here + step[0] + step[1] * turn) % 4
    row = iota((ROWS, 1), 0)
    piece = row // (2 * SHARE)
    move = jnp.where(piece == 0, FAR[0], jnp.where(piece == 1, turn, jnp.where(piece == 2, -turn, 0)))
    lane = (there + move + 4) % 4 * other_stride + target * first_stride + row // 2 % SHARE
    quarters = (row % 2).astype(F32) * 0.25
    return picked(columns, lane, wave.astype(F32) / MODULUS, quarters)


def phase_rows(p, shots_ref, lhs, start, stop):
    for k in range(start, stop, 256):
        lhs[:, k : k + 256] = cosine(jnp.dot(p, shots_ref[:, k : k + 256], preferred_element_type=F32)).astype(BF16)


def first_kernel(place_ref, ray_ref, grid_ref, x_ref, out, data_ref, shots_ref, lhs, total, buf, ray_buf, grid_buf, sems):
    small = [pltpu.make_async_copy(ray_ref, ray_buf, sems.at[8]), pltpu.make_async_copy(grid_ref, grid_buf, sems.at[9])]
    for copy in small:
        copy.start()
    part = LOCAL // 8
    copies = []
    for i in range(8):
        at = pl.ds(i * part, part)
        copies.append(pltpu.make_async_copy(x_ref.at[at], buf.at[at], sems.at[i]))
        copies[-1].start()
    for copy in small:
        copy.wait()
    grid_rows(grid_buf, shots_ref)
    p = chosen_rows(FAR, place_ref, ray_columns(ray_buf))
    half = DEPTH // 2
    phase_rows(p, shots_ref, lhs, 0, half)
    for step in range(2):
        for i in range(4 * step, 4 * step + 4):
            copies[i].wait()
            for s in range(i * part, (i + 1) * part, 8):
                data_ref[2 * s : 2 * s + 16] = buf[s : s + 8].reshape(16, WIDTH)
        depth = slice(step * half, (step + 1) * half)
        for n in range(0, WIDTH, 256):
            if step == 0:
                phase_rows(p, shots_ref, lhs, half + n, half + n + 256)
            r = jnp.dot(lhs[:, depth], data_ref[depth, n : n + 256], preferred_element_type=F32)
            if step == 0:
                total[:, n : n + 256] = r
            else:
                out[:, n : n + 256] = (r + total[:, n : n + 256]).astype(out.dtype)


def first(spot, ray_table, shot_grid, data):
    held = [pltpu.with_memory_space_constraint(a, pltpu.HBM) for a in (ray_table, shot_grid, data)]
    return pl.pallas_call(
        first_kernel,
        out_shape=[jax.ShapeDtypeStruct((n, m), BF16) for n, m in ((ROWS, WIDTH), (DEPTH, WIDTH), (8, DEPTH))],
        in_specs=[SMEM, HBM, HBM, HBM],
        out_specs=[VMEM] * 3,
        scratch_shapes=[
            pltpu.VMEM((ROWS, DEPTH), BF16),
            pltpu.VMEM((ROWS, WIDTH), F32),
            pltpu.VMEM((LOCAL, 2, WIDTH), BF16),
            pltpu.VMEM((2, RAYS), jnp.int32),
            pltpu.VMEM((2, LOCAL), jnp.int32),
            pltpu.SemaphoreType.DMA((10,)),
        ],
        compiler_params=pltpu.CompilerParams(vmem_limit_bytes=20 * 2**20),
        cost_estimate=pl.CostEstimate(flops=2 * ROWS * DEPTH * WIDTH, bytes_accessed=8 * 2**20, transcendentals=0),
        name="encode_first",
    )(spot, *held)


def later_kernel(steps, place_ref, ray_ref, shots_ref, data_ref, *refs):
    outs, lhs = refs[: len(steps)], refs[len(steps) :]
    columns = ray_columns(ray_ref)
    ps = [chosen_rows(step, place_ref, columns) for step in steps]
    phase_rows(ps[0], shots_ref, lhs[0], 0, DEPTH)
    for i, out in enumerate(outs):
        for n in range(4):
            if i + 1 < len(outs):
                phase_rows(ps[i + 1], shots_ref, lhs[i + 1], n * DEPTH // 4, (n + 1) * DEPTH // 4)
            at = slice(n * 256, (n + 1) * 256)
            out[:, at] = jnp.dot(lhs[i][...], data_ref[:, at], preferred_element_type=F32).astype(out.dtype)


def own_kernel(place_ref, ray_ref, shots_ref, data_ref, rcv_ref, out, cos_ref, sin_ref, lhs):
    later_kernel((HERE,), place_ref, ray_ref, shots_ref, data_ref, out, lhs)
    row = iota((2 * SHARE, 1), 0)
    row8 = iota((8, WIDTH), 0)
    grid = jnp.where(row8 < 2, rcv_ref[0:1, :], jnp.where(row8 < 4, rcv_ref[1:2, :], 0)).astype(F32).astype(BF16)
    lane = place_ref[0] * (RAYS // ZH) + place_ref[1] * SHARE + row // 2
    p = picked(ray_columns(ray_ref), lane, place_ref[3].astype(F32) / MODULUS, 0.0)
    for i in range(0, WIDTH, 256):
        at = slice(i, i + 256)
        c, s = cos_minus_sin(jnp.dot(p, grid[:, at], preferred_element_type=F32))
        cos_ref[:, at] = SCALE * c
        sin_ref[:, at] = jnp.where(row % 2 == 0, SCALE * s, -SCALE * s)


def later(steps, dtypes, spot, ray_table, shots, data, *more):
    shapes = [jax.ShapeDtypeStruct((ROWS, WIDTH), dtype) for dtype in dtypes]
    if more:
        shapes += [jax.ShapeDtypeStruct((2 * SHARE, WIDTH), F32)] * 2
    return pl.pallas_call(
        own_kernel if more else functools.partial(later_kernel, steps),
        out_shape=shapes,
        in_specs=[SMEM] + [VMEM] * (3 + len(more)),
        out_specs=[VMEM] * len(shapes),
        scratch_shapes=[pltpu.VMEM((ROWS, DEPTH), BF16)] * len(steps),
        compiler_params=pltpu.CompilerParams(vmem_limit_bytes=20 * 2**20),
        cost_estimate=pl.CostEstimate(flops=2 * len(steps) * ROWS * DEPTH * WIDTH, bytes_accessed=8 * 2**20, transcendentals=0),
        name="encode_later",
    )(spot, ray_table, shots, data, *more)


def add_kernel(own, *refs):
    total = own[...]
    for piece in refs[:-1]:
        total = total + piece[...].astype(F32)
    refs[-1][...] = total.astype(BF16)


def add(own, *pieces):
    return pl.pallas_call(
        add_kernel,
        out_shape=jax.ShapeDtypeStruct(own.shape, BF16),
        in_specs=[VMEM] * (1 + len(pieces)),
        out_specs=VMEM,
        compiler_params=pltpu.CompilerParams(vmem_limit_bytes=8 * 2**20),
        name="add",
    )(own, *pieces)


def spread_kernel(own, back, near, *outs):
    unit = own.shape[0] // 4
    for k, out in enumerate(outs):
        at = slice(k * unit, (k + 1) * unit)
        out[...] = (own[at, :] + back[at, :].astype(F32) + near[at, :].astype(F32)).astype(out.dtype)


def spread(own, back, near):
    unit = own.shape[0] // 4
    return pl.pallas_call(
        spread_kernel,
        out_shape=[jax.ShapeDtypeStruct((unit, WIDTH), dtype) for dtype in (BF16, BF16, BF16, F32)],
        in_specs=[VMEM] * 3,
        out_specs=[VMEM] * 4,
        compiler_params=pltpu.CompilerParams(vmem_limit_bytes=8 * 2**20),
        name="spread",
    )(own, back, near)


def last_kernel(own, far, near, back, cos_ref, sin_ref, out):
    count = own.shape[0]
    real = iota((count, 1), 0) % 2 == 0
    for i in range(0, WIDTH, 256):
        at = slice(i, i + 256)
        total = own[:, at] + far[:, at].astype(F32) + near[:, at].astype(F32) + back[:, at].astype(F32)
        crossed = jnp.where(real, pltpu.roll(total, count - 1, 0), pltpu.roll(total, 1, 0))
        out[:, at] = (total * cos_ref[:, at] + crossed * sin_ref[:, at]).astype(BF16)


def last(*args):
    return pl.pallas_call(
        last_kernel,
        out_shape=jax.ShapeDtypeStruct((2 * SHARE, WIDTH), BF16),
        in_specs=[VMEM] * 6,
        out_specs=VMEM,
        compiler_params=pltpu.CompilerParams(vmem_limit_bytes=8 * 2**20),
        name="last",
    )(*args)


def send(value, leg, step):
    pairs = []
    for index in range(ZH * XS * RCV):
        zh, x, rcv = index // (XS * RCV), index // RCV % XS, index % RCV
        move = step[0] + step[1] * (1 - rcv // (RCV // 2) * 2)
        if (rcv % CORES == 0) == (leg == 0):
            x = (x + move) % XS
        else:
            zh = (zh + move) % ZH
        pairs.append((index, (zh * XS + x) * RCV + rcv))
    return lax.ppermute(value, ("z_hi", "x", "rcv"), pairs)


def on_device(spectra, shot_grid, ray_table, receiver_grid):
    zh, x, rcv = (lax.axis_index(name) for name in ("z_hi", "x", "rcv"))
    first_x = rcv % CORES == 0
    turn = 1 - rcv // (RCV // 2) * 2
    along_x, along_z = SHARE, RAYS // ZH
    spot = [zh, x, jnp.where(first_x, x, zh), BASE + rcv, turn]
    spot += [jnp.where(first_x, along_x, along_z), jnp.where(first_x, along_z, along_x), jnp.where(first_x, zh, x)]
    spot = jnp.stack(spot).astype(jnp.int32)
    far, data, shots = first(spot, ray_table, shot_grid, spectra.reshape(LOCAL, 2, WIDTH))
    relayed = send(far, 0, NEAR)
    back, near = later([BACK, NEAR], [BF16, F32], spot, ray_table, shots, data)
    from_back = send(back, 0, BACK)
    from_near = send(add(near, relayed), 0, NEAR)
    shots, back = lax.optimization_barrier((shots, back))
    here, cosines, sines = later([HERE], [F32], spot, ray_table, shots, data, receiver_grid)
    far, near, back, here = spread(here, from_back, from_near)
    pieces = [send(far, 1, FAR), send(near, 1, NEAR), send(back, 1, BACK)]
    turned = last(here, *pieces, cosines, sines)
    return lax.all_to_all(turned.reshape(SHARE, 1, 2, WIDTH), "rcv", split_axis=0, concat_axis=1, tiled=True)


def solution(mesh):
    split = Mesh(mesh.devices.reshape(ZH, XS, RCV), ("z_hi", "x", "rcv"))
    in_specs = (P("rcv", ("z_hi", "x"), None, None), P(None, ("z_hi", "x")), P(), P())
    out_specs = P(("z_hi", "x", "rcv"), None, None, None)
    return jax.shard_map(on_device, mesh=split, in_specs=in_specs, out_specs=out_specs, check_vma=False)
```

```python
import functools
import math

import jax
import jax.numpy as jnp
import numpy as np
from jax import lax
from jax.experimental import pallas as pl
from jax.experimental.pallas import tpu as pltpu
from jax.sharding import Mesh
from jax.sharding import PartitionSpec as P

BASE = 5
MODULUS = 1024
ZH, XS, RCV, CORES = 4, 4, 16, 2
RAYS, WIDTH, LOCAL = 512, 1024, 1024
SHARE = RAYS // (ZH * XS)
ROWS = 2 * ZH * SHARE
DEPTH = 2 * LOCAL
VMEM = pl.BlockSpec(memory_space=pltpu.VMEM)
SMEM = pl.BlockSpec(memory_space=pltpu.SMEM)
HBM = pl.BlockSpec(memory_space=pltpu.HBM)
FAR, NEAR, BACK, HERE = (2, 0), (0, 1), (0, -1), (0, 0)
SCALE = 1.0 / math.sqrt(LOCAL * ZH * XS)
F32, BF16 = jnp.float32, jnp.bfloat16


def fitted(fn, degree):
    points = 0.125 * (1 + np.cos(np.pi * (np.arange(400) + 0.5) / 400))
    series = np.polynomial.chebyshev.Chebyshev.fit(points, fn(np.sqrt(points)), degree, domain=[0, 0.25])
    return [float(a) for a in series.convert(kind=np.polynomial.Polynomial).coef]


HALF_COS = fitted(lambda f: np.cos(np.pi * f), 4)
HALF_SIN = fitted(lambda f: np.sin(np.pi * f) / f, 4)
ROOT_SIN = fitted(lambda f: math.sqrt(2.0) * np.sin(np.pi * f) / f, 4)


def horner(coefs, v):
    total = v * coefs[-1] + coefs[-2]
    for a in coefs[-3::-1]:
        total = total * v + a
    return total


def cosine(turns):
    f = turns - jnp.round(turns)
    t = f * horner(ROOT_SIN, f * f)
    return 1.0 - t * t


def cos_minus_sin(turns):
    f = turns - jnp.round(turns)
    v = f * f
    s = f * horner(HALF_SIN, v)
    twice = s * -2.0
    return twice * s + 1.0, twice * horner(HALF_COS, v)


def iota(shape, axis):
    return lax.broadcasted_iota(jnp.int32, shape, axis)


def ray_columns(ray_ref):
    row = iota((8, RAYS), 0)
    r0, r1 = ray_ref[0:1, :].astype(F32), ray_ref[1:2, :].astype(F32)
    return jnp.where(row < 2, r0, jnp.where(row < 4, r1, jnp.where(row == 4, 1.0, 0.0))).astype(BF16)


def picked(columns, lane_of_row, turn, quarters):
    rows = lane_of_row.shape[0]
    chosen = (iota((rows, RAYS), 1) == lane_of_row).astype(BF16)
    p = lax.dot_general(chosen, columns, (((1,), (1,)), ((), ())), preferred_element_type=F32)
    col = iota((rows, 8), 1)
    p = jnp.where(col < 4, p * turn, p)
    high = p.astype(BF16).astype(F32)
    p = jnp.where((col == 1) | (col == 3), p - high, high)
    return jnp.where(col == 5, quarters, p).astype(BF16)


def grid_rows(grid_ref, shots_ref):
    row = iota((8, LOCAL), 0)
    g = jnp.where(row < 2, grid_ref[0:1, :], jnp.where(row < 4, grid_ref[1:2, :], 0)).astype(F32).astype(BF16)
    twice = (iota((128, 256), 0) == iota((128, 256), 1) // 2).astype(BF16)
    rest = iota((8, 256), 0)
    rest = jnp.where(rest == 4, (iota((8, 256), 1) % 2).astype(F32) * -0.25, jnp.where(rest == 5, 1.0, 0.0))
    for i in range(LOCAL // 128):
        wide = jnp.dot(g[:, i * 128 : (i + 1) * 128], twice, preferred_element_type=F32) + rest
        shots_ref[:, i * 256 : (i + 1) * 256] = wide.astype(BF16)


def chosen_rows(step, place_ref, columns):
    here, wave, turn, first_stride, other_stride, there = (place_ref[k] for k in (2, 3, 4, 5, 6, 7))
    target = (here + step[0] + step[1] * turn) % 4
    row = iota((ROWS, 1), 0)
    piece = row // (2 * SHARE)
    move = jnp.where(piece == 0, FAR[0], jnp.where(piece == 1, turn, jnp.where(piece == 2, -turn, 0)))
    lane = (there + move + 4) % 4 * other_stride + target * first_stride + row // 2 % SHARE
    quarters = (row % 2).astype(F32) * 0.25
    return picked(columns, lane, wave.astype(F32) / MODULUS, quarters)


def phase_rows(p, shots_ref, lhs, start, stop):
    for k in range(start, stop, 256):
        lhs[:, k : k + 256] = cosine(jnp.dot(p, shots_ref[:, k : k + 256], preferred_element_type=F32)).astype(BF16)


def first_kernel(place_ref, ray_ref, grid_ref, x_ref, out, data_ref, shots_ref, lhs, total, buf, ray_buf, grid_buf, sems):
    small = [pltpu.make_async_copy(ray_ref, ray_buf, sems.at[8]), pltpu.make_async_copy(grid_ref, grid_buf, sems.at[9])]
    for copy in small:
        copy.start()
    part = LOCAL // 8
    copies = []
    for i in range(8):
        at = pl.ds(i * part, part)
        copies.append(pltpu.make_async_copy(x_ref.at[at], buf.at[at], sems.at[i]))
        copies[-1].start()
    for copy in small:
        copy.wait()
    grid_rows(grid_buf, shots_ref)
    p = chosen_rows(FAR, place_ref, ray_columns(ray_buf))
    half = DEPTH // 2
    phase_rows(p, shots_ref, lhs, 0, half)
    for step in range(2):
        for i in range(4 * step, 4 * step + 4):
            copies[i].wait()
            for s in range(i * part, (i + 1) * part, 8):
                data_ref[2 * s : 2 * s + 16] = buf[s : s + 8].reshape(16, WIDTH)
        depth = slice(step * half, (step + 1) * half)
        for n in range(0, WIDTH, 256):
            if step == 0:
                phase_rows(p, shots_ref, lhs, half + n, half + n + 256)
            r = jnp.dot(lhs[:, depth], data_ref[depth, n : n + 256], preferred_element_type=F32)
            if step == 0:
                total[:, n : n + 256] = r
            else:
                out[:, n : n + 256] = (r + total[:, n : n + 256]).astype(out.dtype)


def first(spot, ray_table, shot_grid, data):
    held = [pltpu.with_memory_space_constraint(a, pltpu.HBM) for a in (ray_table, shot_grid, data)]
    return pl.pallas_call(
        first_kernel,
        out_shape=[jax.ShapeDtypeStruct((n, m), BF16) for n, m in ((ROWS, WIDTH), (DEPTH, WIDTH), (8, DEPTH))],
        in_specs=[SMEM, HBM, HBM, HBM],
        out_specs=[VMEM] * 3,
        scratch_shapes=[
            pltpu.VMEM((ROWS, DEPTH), BF16),
            pltpu.VMEM((ROWS, WIDTH), F32),
            pltpu.VMEM((LOCAL, 2, WIDTH), BF16),
            pltpu.VMEM((2, RAYS), jnp.int32),
            pltpu.VMEM((2, LOCAL), jnp.int32),
            pltpu.SemaphoreType.DMA((10,)),
        ],
        compiler_params=pltpu.CompilerParams(vmem_limit_bytes=20 * 2**20),
        cost_estimate=pl.CostEstimate(flops=2 * ROWS * DEPTH * WIDTH, bytes_accessed=8 * 2**20, transcendentals=0),
        name="encode_first",
    )(spot, *held)


def later_kernel(steps, place_ref, ray_ref, shots_ref, data_ref, *refs):
    outs, lhs = refs[: len(steps)], refs[len(steps) :]
    columns = ray_columns(ray_ref)
    ps = [chosen_rows(step, place_ref, columns) for step in steps]
    phase_rows(ps[0], shots_ref, lhs[0], 0, DEPTH)
    for i, out in enumerate(outs):
        for n in range(4):
            if i + 1 < len(outs):
                phase_rows(ps[i + 1], shots_ref, lhs[i + 1], n * DEPTH // 4, (n + 1) * DEPTH // 4)
            at = slice(n * 256, (n + 1) * 256)
            out[:, at] = jnp.dot(lhs[i][...], data_ref[:, at], preferred_element_type=F32).astype(out.dtype)


def own_kernel(place_ref, ray_ref, shots_ref, data_ref, rcv_ref, out, cos_ref, sin_ref, lhs):
    later_kernel((HERE,), place_ref, ray_ref, shots_ref, data_ref, out, lhs)
    row = iota((2 * SHARE, 1), 0)
    row8 = iota((8, WIDTH), 0)
    grid = jnp.where(row8 < 2, rcv_ref[0:1, :], jnp.where(row8 < 4, rcv_ref[1:2, :], 0)).astype(F32).astype(BF16)
    lane = place_ref[0] * (RAYS // ZH) + place_ref[1] * SHARE + row // 2
    p = picked(ray_columns(ray_ref), lane, place_ref[3].astype(F32) / MODULUS, 0.0)
    for i in range(0, WIDTH, 256):
        at = slice(i, i + 256)
        c, s = cos_minus_sin(jnp.dot(p, grid[:, at], preferred_element_type=F32))
        cos_ref[:, at] = SCALE * c
        sin_ref[:, at] = jnp.where(row % 2 == 0, SCALE * s, -SCALE * s)


def later(steps, dtypes, spot, ray_table, shots, data, *more):
    shapes = [jax.ShapeDtypeStruct((ROWS, WIDTH), dtype) for dtype in dtypes]
    if more:
        shapes += [jax.ShapeDtypeStruct((2 * SHARE, WIDTH), F32)] * 2
    return pl.pallas_call(
        own_kernel if more else functools.partial(later_kernel, steps),
        out_shape=shapes,
        in_specs=[SMEM] + [VMEM] * (3 + len(more)),
        out_specs=[VMEM] * len(shapes),
        scratch_shapes=[pltpu.VMEM((ROWS, DEPTH), BF16)] * len(steps),
        compiler_params=pltpu.CompilerParams(vmem_limit_bytes=20 * 2**20),
        cost_estimate=pl.CostEstimate(flops=2 * len(steps) * ROWS * DEPTH * WIDTH, bytes_accessed=8 * 2**20, transcendentals=0),
        name="encode_later",
    )(spot, ray_table, shots, data, *more)


def add_kernel(own, *refs):
    total = own[...]
    for piece in refs[:-1]:
        total = total + piece[...].astype(F32)
    refs[-1][...] = total.astype(BF16)


def add(own, *pieces):
    return pl.pallas_call(
        add_kernel,
        out_shape=jax.ShapeDtypeStruct(own.shape, BF16),
        in_specs=[VMEM] * (1 + len(pieces)),
        out_specs=VMEM,
        compiler_params=pltpu.CompilerParams(vmem_limit_bytes=8 * 2**20),
        name="add",
    )(own, *pieces)


def spread_kernel(own, back, near, *outs):
    unit = own.shape[0] // 4
    for k, out in enumerate(outs):
        at = slice(k * unit, (k + 1) * unit)
        out[...] = (own[at, :] + back[at, :].astype(F32) + near[at, :].astype(F32)).astype(out.dtype)


def spread(own, back, near):
    unit = own.shape[0] // 4
    return pl.pallas_call(
        spread_kernel,
        out_shape=[jax.ShapeDtypeStruct((unit, WIDTH), dtype) for dtype in (BF16, BF16, BF16, F32)],
        in_specs=[VMEM] * 3,
        out_specs=[VMEM] * 4,
        compiler_params=pltpu.CompilerParams(vmem_limit_bytes=8 * 2**20),
        name="spread",
    )(own, back, near)


def last_kernel(own, far, near, back, cos_ref, sin_ref, out):
    count = own.shape[0]
    real = iota((count, 1), 0) % 2 == 0
    for i in range(0, WIDTH, 256):
        at = slice(i, i + 256)
        total = own[:, at] + far[:, at].astype(F32) + near[:, at].astype(F32) + back[:, at].astype(F32)
        crossed = jnp.where(real, pltpu.roll(total, count - 1, 0), pltpu.roll(total, 1, 0))
        out[:, at] = (total * cos_ref[:, at] + crossed * sin_ref[:, at]).astype(BF16)


def last(*args):
    return pl.pallas_call(
        last_kernel,
        out_shape=jax.ShapeDtypeStruct((2 * SHARE, WIDTH), BF16),
        in_specs=[VMEM] * 6,
        out_specs=VMEM,
        compiler_params=pltpu.CompilerParams(vmem_limit_bytes=8 * 2**20),
        name="last",
    )(*args)


def send(value, leg, step):
    pairs = []
    for index in range(ZH * XS * RCV):
        zh, x, rcv = index // (XS * RCV), index // RCV % XS, index % RCV
        move = step[0] + step[1] * (1 if rcv % CORES == 0 else 1 - rcv // (RCV // 2) * 2)
        if (rcv % CORES == 0) == (leg == 0):
            x = (x + move) % XS
        else:
            zh = (zh + move) % ZH
        pairs.append((index, (zh * XS + x) * RCV + rcv))
    return lax.ppermute(value, ("z_hi", "x", "rcv"), pairs)


def on_device(spectra, shot_grid, ray_table, receiver_grid):
    zh, x, rcv = (lax.axis_index(name) for name in ("z_hi", "x", "rcv"))
    first_x = rcv % CORES == 0
    turn = jnp.where(first_x, 1, 1 - rcv // (RCV // 2) * 2)
    along_x, along_z = SHARE, RAYS // ZH
    spot = [zh, x, jnp.where(first_x, x, zh), BASE + rcv, turn]
    spot += [jnp.where(first_x, along_x, along_z), jnp.where(first_x, along_z, along_x), jnp.where(first_x, zh, x)]
    spot = jnp.stack(spot).astype(jnp.int32)
    far, data, shots = first(spot, ray_table, shot_grid, spectra.reshape(LOCAL, 2, WIDTH))
    relayed = send(far, 0, NEAR)
    back, near = later([BACK, NEAR], [BF16, F32], spot, ray_table, shots, data)
    from_back = send(back, 0, BACK)
    from_near = send(add(near, relayed), 0, NEAR)
    shots, back = lax.optimization_barrier((shots, back))
    here, cosines, sines = later([HERE], [F32], spot, ray_table, shots, data, receiver_grid)
    far, near, back, here = spread(here, from_back, from_near)
    pieces = [send(far, 1, FAR), send(near, 1, NEAR), send(back, 1, BACK)]
    turned = last(here, *pieces, cosines, sines)
    return lax.all_to_all(turned.reshape(SHARE, 1, 2, WIDTH), "rcv", split_axis=0, concat_axis=1, tiled=True)


def solution(mesh):
    split = Mesh(mesh.devices.reshape(ZH, XS, RCV), ("z_hi", "x", "rcv"))
    in_specs = (P("rcv", ("z_hi", "x"), None, None), P(None, ("z_hi", "x")), P(), P())
    out_specs = P(("z_hi", "x", "rcv"), None, None, None)
    return jax.shard_map(on_device, mesh=split, in_specs=in_specs, out_specs=out_specs, check_vma=False)
```

```python
import functools
import math

import jax
import jax.numpy as jnp
import numpy as np
from jax import lax
from jax.experimental import pallas as pl
from jax.experimental.pallas import tpu as pltpu
from jax.sharding import Mesh
from jax.sharding import PartitionSpec as P

BASE = 5
MODULUS = 1024
ZH, XS, RCV, CORES = 4, 4, 16, 2
RAYS, WIDTH, LOCAL = 512, 1024, 1024
SHARE = RAYS // (ZH * XS)
ROWS = 2 * ZH * SHARE
DEPTH = 2 * LOCAL
VMEM = pl.BlockSpec(memory_space=pltpu.VMEM)
SMEM = pl.BlockSpec(memory_space=pltpu.SMEM)
HBM = pl.BlockSpec(memory_space=pltpu.HBM)
FAR, NEAR, BACK, HERE = (2, 0), (0, 1), (0, -1), (0, 0)
SCALE = 1.0 / math.sqrt(LOCAL * ZH * XS)
F32, BF16 = jnp.float32, jnp.bfloat16


def fitted(fn, degree):
    points = 0.125 * (1 + np.cos(np.pi * (np.arange(400) + 0.5) / 400))
    series = np.polynomial.chebyshev.Chebyshev.fit(points, fn(np.sqrt(points)), degree, domain=[0, 0.25])
    return [float(a) for a in series.convert(kind=np.polynomial.Polynomial).coef]


HALF_COS = fitted(lambda f: np.cos(np.pi * f), 4)
HALF_SIN = fitted(lambda f: np.sin(np.pi * f) / f, 4)
ROOT_SIN = fitted(lambda f: math.sqrt(2.0) * np.sin(np.pi * f) / f, 4)


def horner(coefs, v):
    total = v * coefs[-1] + coefs[-2]
    for a in coefs[-3::-1]:
        total = total * v + a
    return total


def cosine(turns):
    f = turns - jnp.round(turns)
    t = f * horner(ROOT_SIN, f * f)
    return 1.0 - t * t


def cos_minus_sin(turns):
    f = turns - jnp.round(turns)
    v = f * f
    s = f * horner(HALF_SIN, v)
    twice = s * -2.0
    return twice * s + 1.0, twice * horner(HALF_COS, v)


def iota(shape, axis):
    return lax.broadcasted_iota(jnp.int32, shape, axis)


def ray_columns(ray_ref):
    row = iota((8, RAYS), 0)
    r0, r1 = ray_ref[0:1, :].astype(F32), ray_ref[1:2, :].astype(F32)
    return jnp.where(row < 2, r0, jnp.where(row < 4, r1, jnp.where(row == 4, 1.0, 0.0))).astype(BF16)


def picked(columns, lane_of_row, turn, quarters):
    rows = lane_of_row.shape[0]
    chosen = (iota((rows, RAYS), 1) == lane_of_row).astype(BF16)
    p = lax.dot_general(chosen, columns, (((1,), (1,)), ((), ())), preferred_element_type=F32)
    col = iota((rows, 8), 1)
    p = jnp.where(col < 4, p * turn, p)
    high = p.astype(BF16).astype(F32)
    p = jnp.where((col == 1) | (col == 3), p - high, high)
    return jnp.where(col == 5, quarters, p).astype(BF16)


def grid_rows(grid_ref, shots_ref):
    row = iota((8, LOCAL), 0)
    g = jnp.where(row < 2, grid_ref[0:1, :], jnp.where(row < 4, grid_ref[1:2, :], 0)).astype(F32).astype(BF16)
    twice = (iota((128, 256), 0) == iota((128, 256), 1) // 2).astype(BF16)
    rest = iota((8, 256), 0)
    rest = jnp.where(rest == 4, (iota((8, 256), 1) % 2).astype(F32) * -0.25, jnp.where(rest == 5, 1.0, 0.0))
    for i in range(LOCAL // 128):
        wide = jnp.dot(g[:, i * 128 : (i + 1) * 128], twice, preferred_element_type=F32) + rest
        shots_ref[:, i * 256 : (i + 1) * 256] = wide.astype(BF16)


def chosen_rows(step, place_ref, columns):
    here, wave, turn, first_stride, other_stride, there = (place_ref[k] for k in (2, 3, 4, 5, 6, 7))
    target = (here + step[0] + step[1] * turn) % 4
    row = iota((ROWS, 1), 0)
    piece = row // (2 * SHARE)
    move = jnp.where(piece == 0, FAR[0], jnp.where(piece == 1, turn, jnp.where(piece == 2, -turn, 0)))
    lane = (there + move + 4) % 4 * other_stride + target * first_stride + row // 2 % SHARE
    quarters = (row % 2).astype(F32) * 0.25
    return picked(columns, lane, wave.astype(F32) / MODULUS, quarters)


def phase_rows(p, shots_ref, lhs, start, stop):
    for k in range(start, stop, 256):
        lhs[:, k : k + 256] = cosine(jnp.dot(p, shots_ref[:, k : k + 256], preferred_element_type=F32)).astype(BF16)


def first_kernel(place_ref, ray_ref, grid_ref, x_ref, out, data_ref, shots_ref, lhs, total, buf, ray_buf, grid_buf, sems):
    small = [pltpu.make_async_copy(ray_ref, ray_buf, sems.at[8]), pltpu.make_async_copy(grid_ref, grid_buf, sems.at[9])]
    for copy in small:
        copy.start()
    part = LOCAL // 8
    copies = []
    for i in range(8):
        at = pl.ds(i * part, part)
        copies.append(pltpu.make_async_copy(x_ref.at[at], buf.at[at], sems.at[i]))
        copies[-1].start()
    for copy in small:
        copy.wait()
    grid_rows(grid_buf, shots_ref)
    p = chosen_rows(FAR, place_ref, ray_columns(ray_buf))
    half = DEPTH // 2
    phase_rows(p, shots_ref, lhs, 0, half)
    for step in range(2):
        for i in range(4 * step, 4 * step + 4):
            copies[i].wait()
            for s in range(i * part, (i + 1) * part, 8):
                data_ref[2 * s : 2 * s + 16] = buf[s : s + 8].reshape(16, WIDTH)
        depth = slice(step * half, (step + 1) * half)
        for n in range(0, WIDTH, 256):
            if step == 0:
                phase_rows(p, shots_ref, lhs, half + n, half + n + 256)
            r = jnp.dot(lhs[:, depth], data_ref[depth, n : n + 256], preferred_element_type=F32)
            if step == 0:
                total[:, n : n + 256] = r
            else:
                out[:, n : n + 256] = (r + total[:, n : n + 256]).astype(out.dtype)


def first(spot, ray_table, shot_grid, data):
    held = [pltpu.with_memory_space_constraint(a, pltpu.HBM) for a in (ray_table, shot_grid, data)]
    return pl.pallas_call(
        first_kernel,
        out_shape=[jax.ShapeDtypeStruct((n, m), BF16) for n, m in ((ROWS, WIDTH), (DEPTH, WIDTH), (8, DEPTH))],
        in_specs=[SMEM, HBM, HBM, HBM],
        out_specs=[VMEM] * 3,
        scratch_shapes=[
            pltpu.VMEM((ROWS, DEPTH), BF16),
            pltpu.VMEM((ROWS, WIDTH), F32),
            pltpu.VMEM((LOCAL, 2, WIDTH), BF16),
            pltpu.VMEM((2, RAYS), jnp.int32),
            pltpu.VMEM((2, LOCAL), jnp.int32),
            pltpu.SemaphoreType.DMA((10,)),
        ],
        compiler_params=pltpu.CompilerParams(vmem_limit_bytes=20 * 2**20),
        cost_estimate=pl.CostEstimate(flops=2 * ROWS * DEPTH * WIDTH, bytes_accessed=8 * 2**20, transcendentals=0),
        name="encode_first",
    )(spot, *held)


def later_kernel(steps, place_ref, ray_ref, shots_ref, data_ref, *refs):
    outs, lhs = refs[: len(steps)], refs[len(steps) :]
    columns = ray_columns(ray_ref)
    ps = [chosen_rows(step, place_ref, columns) for step in steps]
    phase_rows(ps[0], shots_ref, lhs[0], 0, DEPTH)
    for i, out in enumerate(outs):
        for n in range(4):
            if i + 1 < len(outs):
                phase_rows(ps[i + 1], shots_ref, lhs[i + 1], n * DEPTH // 4, (n + 1) * DEPTH // 4)
            at = slice(n * 256, (n + 1) * 256)
            out[:, at] = jnp.dot(lhs[i][...], data_ref[:, at], preferred_element_type=F32).astype(out.dtype)


def own_kernel(place_ref, ray_ref, shots_ref, data_ref, rcv_ref, out, cos_ref, sin_ref, lhs):
    later_kernel((HERE,), place_ref, ray_ref, shots_ref, data_ref, out, lhs)
    row = iota((2 * SHARE, 1), 0)
    row8 = iota((8, WIDTH), 0)
    grid = jnp.where(row8 < 2, rcv_ref[0:1, :], jnp.where(row8 < 4, rcv_ref[1:2, :], 0)).astype(F32).astype(BF16)
    lane = place_ref[0] * (RAYS // ZH) + place_ref[1] * SHARE + row // 2
    p = picked(ray_columns(ray_ref), lane, place_ref[3].astype(F32) / MODULUS, 0.0)
    for i in range(0, WIDTH, 256):
        at = slice(i, i + 256)
        c, s = cos_minus_sin(jnp.dot(p, grid[:, at], preferred_element_type=F32))
        cos_ref[:, at] = SCALE * c
        sin_ref[:, at] = jnp.where(row % 2 == 0, SCALE * s, -SCALE * s)


def later(steps, dtypes, spot, ray_table, shots, data, *more):
    shapes = [jax.ShapeDtypeStruct((ROWS, WIDTH), dtype) for dtype in dtypes]
    if more:
        shapes += [jax.ShapeDtypeStruct((2 * SHARE, WIDTH), F32)] * 2
    return pl.pallas_call(
        own_kernel if more else functools.partial(later_kernel, steps),
        out_shape=shapes,
        in_specs=[SMEM] + [VMEM] * (3 + len(more)),
        out_specs=[VMEM] * len(shapes),
        scratch_shapes=[pltpu.VMEM((ROWS, DEPTH), BF16)] * len(steps),
        compiler_params=pltpu.CompilerParams(vmem_limit_bytes=20 * 2**20),
        cost_estimate=pl.CostEstimate(flops=2 * len(steps) * ROWS * DEPTH * WIDTH, bytes_accessed=8 * 2**20, transcendentals=0),
        name="encode_later",
    )(spot, ray_table, shots, data, *more)


def add_kernel(own, *refs):
    total = own[...]
    for piece in refs[:-1]:
        total = total + piece[...].astype(F32)
    refs[-1][...] = total.astype(BF16)


def add(own, *pieces):
    return pl.pallas_call(
        add_kernel,
        out_shape=jax.ShapeDtypeStruct(own.shape, BF16),
        in_specs=[VMEM] * (1 + len(pieces)),
        out_specs=VMEM,
        compiler_params=pltpu.CompilerParams(vmem_limit_bytes=8 * 2**20),
        name="add",
    )(own, *pieces)


def spread_kernel(own, back, near, *outs):
    unit = own.shape[0] // 4
    for k, out in enumerate(outs):
        at = slice(k * unit, (k + 1) * unit)
        out[...] = (own[at, :] + back[at, :].astype(F32) + near[at, :].astype(F32)).astype(out.dtype)


def spread(own, back, near):
    unit = own.shape[0] // 4
    return pl.pallas_call(
        spread_kernel,
        out_shape=[jax.ShapeDtypeStruct((unit, WIDTH), dtype) for dtype in (BF16, BF16, BF16, F32)],
        in_specs=[VMEM] * 3,
        out_specs=[VMEM] * 4,
        compiler_params=pltpu.CompilerParams(vmem_limit_bytes=8 * 2**20),
        name="spread",
    )(own, back, near)


def last_kernel(own, far, near, back, cos_ref, sin_ref, out):
    count = own.shape[0]
    real = iota((count, 1), 0) % 2 == 0
    for i in range(0, WIDTH, 256):
        at = slice(i, i + 256)
        total = own[:, at] + far[:, at].astype(F32) + near[:, at].astype(F32) + back[:, at].astype(F32)
        crossed = jnp.where(real, pltpu.roll(total, count - 1, 0), pltpu.roll(total, 1, 0))
        out[:, at] = (total * cos_ref[:, at] + crossed * sin_ref[:, at]).astype(BF16)


def last(*args):
    return pl.pallas_call(
        last_kernel,
        out_shape=jax.ShapeDtypeStruct((2 * SHARE, WIDTH), BF16),
        in_specs=[VMEM] * 6,
        out_specs=VMEM,
        compiler_params=pltpu.CompilerParams(vmem_limit_bytes=8 * 2**20),
        name="last",
    )(*args)


def send(value, leg, step):
    pairs = []
    for index in range(ZH * XS * RCV):
        zh, x, rcv = index // (XS * RCV), index // RCV % XS, index % RCV
        move = step[0] + step[1] * (1 if rcv % CORES == 0 else 1 - rcv // (RCV // 2) * 2)
        if (rcv % CORES == 0) == (leg == 0):
            x = (x + move) % XS
        else:
            zh = (zh + move) % ZH
        pairs.append((index, (zh * XS + x) * RCV + rcv))
    return lax.ppermute(value, ("z_hi", "x", "rcv"), pairs)


def on_device(spectra, shot_grid, ray_table, receiver_grid):
    zh, x, rcv = (lax.axis_index(name) for name in ("z_hi", "x", "rcv"))
    first_x = rcv % CORES == 0
    turn = jnp.where(first_x, 1, 1 - rcv // (RCV // 2) * 2)
    along_x, along_z = SHARE, RAYS // ZH
    spot = [zh, x, jnp.where(first_x, x, zh), BASE + rcv, turn]
    spot += [jnp.where(first_x, along_x, along_z), jnp.where(first_x, along_z, along_x), jnp.where(first_x, zh, x)]
    spot = jnp.stack(spot).astype(jnp.int32)
    far, data, shots = first(spot, ray_table, shot_grid, spectra.reshape(LOCAL, 2, WIDTH))
    relayed = send(far, 0, NEAR)
    back, near = later([BACK, NEAR], [BF16, F32], spot, ray_table, shots, data)
    from_back = send(back, 0, BACK)
    shots, back = lax.optimization_barrier((shots, back))
    here, cosines, sines = later([HERE], [F32], spot, ray_table, shots, data, receiver_grid)
    near, here = lax.optimization_barrier((near, here))
    from_near = send(add(near, relayed), 0, NEAR)
    far, near, back, here = spread(here, from_back, from_near)
    pieces = [send(far, 1, FAR), send(near, 1, NEAR), send(back, 1, BACK)]
    turned = last(here, *pieces, cosines, sines)
    return lax.all_to_all(turned.reshape(SHARE, 1, 2, WIDTH), "rcv", split_axis=0, concat_axis=1, tiled=True)


def solution(mesh):
    split = Mesh(mesh.devices.reshape(ZH, XS, RCV), ("z_hi", "x", "rcv"))
    in_specs = (P("rcv", ("z_hi", "x"), None, None), P(None, ("z_hi", "x")), P(), P())
    out_specs = P(("z_hi", "x", "rcv"), None, None, None)
    return jax.shard_map(on_device, mesh=split, in_specs=in_specs, out_specs=out_specs, check_vma=False)
```
